32 devices in a mesh: gx: 4 (over y, core), gy: 8 (over z, x).
Axes of the slice: x: 2, y: 2, z: 4, core: 2. Of those that a mesh axis runs over, the one named last changes fastest.
Arguments:
- positions: float32 [4, 8, 5, 3, 128], P('gx', 'gy'), may hold values from 0 to 80, as said below
- polarity: float32 [4, 8, 5, 128], P('gx', 'gy'), may hold values from 0.25 to 1.25
- direct_field: float32 [4, 8, 5, 6, 128], P('gx', 'gy'), may hold values from -30 to 30
- atom_count: int32 [4, 8, 5], P('gx', 'gy'), may hold values from 64 to 128, as said below
- pair_list: int32 [4, 8, 3, 61], P('gx', 'gy'), may hold values from 0 to 4, as said below
- pair_count: int32 [4, 8], P('gx', 'gy'), may hold values from 9 to 61, as said below
Outputs:
- dipoles: float32 [4, 8, 5, 6, 128], P('gx', 'gy')
- residual: float32 [4, 8, 5, 6, 128], P('gx', 'gy')
The draws below stay inside these ranges and needn't reach their ends.
Inputs may be any that keep to these rules, and one draw needn't show every extreme that they name: `positions`: coordinates lie in the device's column, the first two in [0, 8), the third in [0, 80); any two atoms, also of neighbouring columns placed as in the reference program, are at least 1 apart. `atom_count`: every device has one block with all 128 atoms. `pair_list`: for e < pair_count the entry (b, s, c) has s in 0..4; with s = 0, c is b or b + 1, otherwise c is b - 1, b or b + 1, all blocks within 0..4; no entry appears twice; every device lists all its s = 0 entries; entries from pair_count on are zeros. `pair_count`: some device lists all 61 possible entries.
All inputs are finite; a program needn't handle non-finite values.
Results may differ from the reference program's by a relative error of at most 0.003.
Values sent between devices are 32-bit elements; how exact they have to be, the bound alone decides.
A program may use at most 64 MiB of HBM per device.

```python
import math
from functools import partial
import jax
import jax.numpy as jnp
from jax import lax

ATOMS = 128
BLOCKS = 5
ITERS = 2
PAIR_CAP = 61
SLAB_X = 4
SLAB_Y = 8


def draw_positions(key, part):
    full_shape = (SLAB_X, SLAB_Y, BLOCKS, 3, ATOMS)
    atom_index = jnp.arange(ATOMS)
    lattice_x = 2.0 * (atom_index % 4).astype(jnp.float32) + 1.0
    lattice_y = 2.0 * (atom_index // 4 % 4).astype(jnp.float32) + 1.0
    layer_z = 2.0 * (atom_index // 16).astype(jnp.float32) + 1.0
    block_base = (jnp.arange(BLOCKS) * (ATOMS // 8)).astype(jnp.float32)
    lattice_z = block_base[:, None] + layer_z[None, :]
    lattice = jnp.stack([jnp.broadcast_to(lattice_x[None, :], (BLOCKS, ATOMS)), jnp.broadcast_to(lattice_y[None, :], (BLOCKS, ATOMS)), lattice_z], axis=1)
    jitter = jax.random.uniform(key, full_shape, jnp.float32, -0.499, 0.499)
    return lattice[None, None] + jitter


def draw_direct_field(key, part):
    key_base, key_scale = jax.random.split(key)
    full_shape = (SLAB_X, SLAB_Y, BLOCKS, 6, ATOMS)
    fraction_x = jnp.arange(SLAB_X).astype(jnp.float32) / max(SLAB_X - 1, 1)
    fraction_y = jnp.arange(SLAB_Y).astype(jnp.float32) / max(SLAB_Y - 1, 1)
    rising = 1.0 + fraction_x[:, None] + fraction_y[None, :]
    base_noise = jnp.clip(jax.random.normal(key_base, full_shape, jnp.float32), -4.0, 4.0)
    atom_scale = jnp.exp(jax.random.uniform(key_scale, (SLAB_X, SLAB_Y, BLOCKS, 1, ATOMS), jnp.float32, math.log(0.3), math.log(3.0)))
    return 0.3 * base_noise * rising[:, :, None, None, None] * atom_scale


def draw_atom_count(key, part):
    key_count, key_full = jax.random.split(key)
    counts = jax.random.randint(key_count, (SLAB_X, SLAB_Y, BLOCKS), ATOMS // 2, ATOMS + 1)
    full_block = jax.random.randint(key_full, (SLAB_X, SLAB_Y, 1), 0, BLOCKS)
    block_id = jnp.arange(BLOCKS)[None, None, :]
    return jnp.where(block_id == full_block, ATOMS, counts).astype(jnp.int32)


def pair_tables(key):
    base_key = jax.random.fold_in(key, 7)
    key_keep, key_level, key_full, key_order = jax.random.split(base_key, 4)
    candidates = 15 * BLOCKS
    flat_index = jnp.arange(candidates)
    slot_id = flat_index // (3 * BLOCKS)
    block_id = flat_index // 3 % BLOCKS
    other_id = block_id + flat_index % 3 - 1
    valid_pair = (other_id >= 0) & (other_id < BLOCKS) & ((slot_id > 0) | (other_id >= block_id))
    density_level = jax.random.randint(key_level, (SLAB_X, SLAB_Y, 1), 4, 11)
    chance = density_level * density_level
    device_id = jnp.arange(SLAB_X * SLAB_Y).reshape(SLAB_X, SLAB_Y, 1)
    full_device = jax.random.randint(key_full, (), 0, SLAB_X * SLAB_Y)
    chance = jnp.where(device_id == full_device, 100, chance)
    roll_value = jax.random.randint(key_keep, (SLAB_X, SLAB_Y, candidates), 0, 100)
    keep_pair = valid_pair[None, None, :] & ((slot_id[None, None, :] == 0) | (roll_value < chance))
    order_score = jax.random.randint(key_order, (SLAB_X, SLAB_Y, candidates), 0, 65536) * candidates + flat_index[None, None, :]
    order_score = jnp.where(keep_pair, order_score, 65536 * candidates + order_score)
    order_index = jnp.argsort(order_score, axis=-1, stable=True)[:, :, :PAIR_CAP]
    pair_total = jnp.sum(keep_pair.astype(jnp.int32), axis=-1)
    table = jnp.stack([jnp.take(block_id, order_index), jnp.take(slot_id, order_index), jnp.take(other_id, order_index)], axis=2)
    live_rows = jnp.arange(PAIR_CAP)[None, None, None, :] < pair_total[:, :, None, None]
    table = jnp.where(live_rows, table, 0)
    return (table.astype(jnp.int32), pair_total.astype(jnp.int32))


def draw_pair_list(key, part):
    return pair_tables(key)[0]


def draw_pair_count(key, part):
    return pair_tables(key)[1]


def shard_levels(rng, shape, shards, smallest, high):
    gain, own = 1.0, jax.random.fold_in(rng, 6)
    for axis_at, parts in shards:
        heights = jnp.exp(jax.random.uniform(jax.random.fold_in(own, axis_at), (parts,), jnp.float32, smallest / len(shards), high / len(shards)))
        gain = gain * jnp.repeat(heights, shape[axis_at] // parts).reshape([-1 if axis == axis_at else 1 for axis in range(len(shape))])
    return gain


def setup_inputs(seed: int = 0) -> dict:
    seeds = jax.random.split(jax.random.key(seed), 7)
    return {
        "positions": draw_positions(jax.random.fold_in(seeds[6], 71), 0),
        "polarity": jnp.clip(jnp.exp(math.log(1.25) - 1.609438 * jax.random.uniform(seeds[1], (SLAB_X, SLAB_Y, BLOCKS, ATOMS), jnp.float32) ** shard_levels(seeds[1], (SLAB_X, SLAB_Y, BLOCKS, ATOMS), ((0, 4), (1, 8)), -0.2, 0.2)), 0.25, 1.25),
        "direct_field": draw_direct_field(jax.random.fold_in(seeds[6], 71), 0),
        "atom_count": draw_atom_count(jax.random.fold_in(seeds[6], 71), 0),
        "pair_list": draw_pair_list(jax.random.fold_in(seeds[6], 71), 0),
        "pair_count": draw_pair_count(jax.random.fold_in(seeds[6], 71), 0),
    }


thole_factor = 0.39
column_width = 8.0
pair_batch = 8
slot_shift_x = (0.0, 0.0, 1.0, 1.0, 1.0)
slot_shift_y = (0.0, 1.0, -1.0, 0.0, 1.0)
slot_moves = ((0, 0), (0, 1), (1, -1), (1, 0), (1, 1))

def tensor_apply(coef_three, coef_five, deltas, moment, axis_sum):
    if axis_sum == 2:
        moments = [moment[:, member, None, :] for member in range(3)]
    else:
        moments = [moment[:, member, :, None] for member in range(3)]
    project = deltas[0] * moments[0] + deltas[1] * moments[1] + deltas[2] * moments[2]
    scaled = coef_five * project
    return jnp.stack([lax.optimization_barrier(jnp.sum(scaled * deltas[member] - coef_three * moments[member], axis=axis_sum)) for member in range(3)], axis=1)

def pair_fields(geom_i, geom_j, dip_i, dip_j, slot_ids, same_block):
    chosen = (slot_ids[:, None] == jnp.arange(5, dtype=jnp.int32)[None, :]).astype(jnp.float32)
    offset_x = column_width * lax.optimization_barrier(jnp.sum(chosen * jnp.array(slot_shift_x, jnp.float32)[None, :], axis=1))
    offset_y = column_width * lax.optimization_barrier(jnp.sum(chosen * jnp.array(slot_shift_y, jnp.float32)[None, :], axis=1))
    delta_x = geom_j[:, 0, None, :] + offset_x[:, None, None] - geom_i[:, 0, :, None]
    delta_y = geom_j[:, 1, None, :] + offset_y[:, None, None] - geom_i[:, 1, :, None]
    delta_z = geom_j[:, 2, None, :] - geom_i[:, 2, :, None]
    dist_sq = delta_x * delta_x + delta_y * delta_y + delta_z * delta_z
    atom_width = geom_i.shape[2]
    same_atom = jnp.arange(atom_width)[:, None] == jnp.arange(atom_width)[None, :]
    diagonal = same_atom[None, :, :] & same_block[:, None, None]
    dist_sq = jnp.where(diagonal, 1.0, dist_sq)
    inv_dist = lax.rsqrt(dist_sq)
    inv_cube = inv_dist * inv_dist * inv_dist
    root_pol = jnp.sqrt(geom_i[:, 3, :, None] * geom_j[:, 3, None, :])
    damping = thole_factor * dist_sq * jnp.sqrt(dist_sq) / root_pol
    lambda_three = -jnp.expm1(-damping)
    lambda_five = lambda_three - damping * jnp.exp(-damping)
    keep_pair = jnp.where(diagonal, 0.0, 1.0)
    coef_three = keep_pair * lambda_three * inv_cube
    coef_five = keep_pair * 3.0 * lambda_five * inv_cube * inv_dist * inv_dist
    deltas = (delta_x, delta_y, delta_z)
    forward = jnp.concatenate([tensor_apply(coef_three, coef_five, deltas, dip_j[:, 0:3], 2), tensor_apply(coef_three, coef_five, deltas, dip_j[:, 3:6], 2)], axis=1)
    backward = jnp.concatenate([tensor_apply(coef_three, coef_five, deltas, dip_i[:, 0:3], 1), tensor_apply(coef_three, coef_five, deltas, dip_i[:, 3:6], 1)], axis=1)
    return (forward, backward)

def accumulate(geom_stack, dip_stack, entries, pair_total, live_turns, capacity_turns):
    blocks = geom_stack.shape[0] // 5
    atom_width = geom_stack.shape[2]
    targets = jnp.arange(5 * blocks, dtype=jnp.int32)
    padded = jnp.pad(entries, ((0, 0), (0, capacity_turns * pair_batch - entries.shape[1])))

    def one_turn(turn_index, accumulated):
        first_row = (turn_index * pair_batch).astype(jnp.int32)
        group_rows = lax.dynamic_slice_in_dim(padded, first_row, pair_batch, 1)
        own_block = group_rows[0]
        slot_ids = group_rows[1]
        other_block = group_rows[2]
        source = slot_ids * blocks + other_block
        live_rows = (first_row + jnp.arange(pair_batch, dtype=jnp.int32) < pair_total).astype(jnp.float32)
        same_block = (slot_ids == 0) & (own_block == other_block)
        forward, backward = pair_fields(jnp.take(geom_stack, own_block, axis=0), jnp.take(geom_stack, source, axis=0), jnp.take(dip_stack, own_block, axis=0), jnp.take(dip_stack, source, axis=0), slot_ids, same_block)
        to_own = (own_block[:, None] == targets[None, :]).astype(jnp.float32) * live_rows[:, None]
        twoway = live_rows * (1.0 - same_block.astype(jnp.float32))
        to_other = (source[:, None] == targets[None, :]).astype(jnp.float32) * twoway[:, None]
        accumulated = accumulated + jnp.einsum('gt,gca->tca', to_own, forward, precision=lax.Precision.HIGHEST)
        return accumulated + jnp.einsum('gt,gca->tca', to_other, backward, precision=lax.Precision.HIGHEST)
    return lax.fori_loop(0, live_turns, one_turn, jnp.zeros((5 * blocks, 6, atom_width), jnp.float32))

def neighbour_stack(whole_array):
    slot_arrays = [jnp.roll(whole_array, (-moves[0], -moves[1]), axis=(0, 1)) for moves in slot_moves]
    return jnp.stack(slot_arrays, axis=2)

def set_sums(first_vec, second_vec):
    product = (first_vec * second_vec).reshape(SLAB_X, SLAB_Y, BLOCKS, 2, 3, ATOMS)
    return lax.optimization_barrier(jnp.sum(product, axis=(0, 1, 2, 4, 5)))

def spread_sets(values):
    return jnp.repeat(values, 3)[:, None]

def reference(positions, polarity, direct_field, atom_count, pair_list, pair_count):
    atom_mask = (jnp.arange(ATOMS, dtype=jnp.int32)[None, None, None, :] < atom_count[:, :, :, None]).astype(jnp.float32)
    pol_wide = polarity[:, :, :, None, :]
    geometry = jnp.concatenate([positions, pol_wide], axis=3)
    geom_stack = neighbour_stack(geometry).reshape(SLAB_X, SLAB_Y, 5 * BLOCKS, 4, ATOMS)
    capacity_turns = -(-PAIR_CAP // pair_batch)
    per_device = jax.vmap(partial(accumulate, live_turns=capacity_turns, capacity_turns=capacity_turns))

    def one_row(row_data):
        return per_device(row_data[0], row_data[1], row_data[2], row_data[3])

    def operate(search):
        dip_stack = neighbour_stack(search).reshape(SLAB_X, SLAB_Y, 5 * BLOCKS, 6, ATOMS)
        accumulated = lax.map(one_row, (geom_stack, dip_stack, pair_list, pair_count))
        accumulated = accumulated.reshape(SLAB_X, SLAB_Y, 5, BLOCKS, 6, ATOMS)
        own_total = accumulated[:, :, 0]
        for slot_index in range(1, 5):
            own_total = own_total + jnp.roll(accumulated[:, :, slot_index], slot_moves[slot_index], axis=(0, 1))
        return search / pol_wide - own_total * atom_mask[:, :, :, None, :]
    residual = direct_field * atom_mask[:, :, :, None, :]
    dipoles = jnp.zeros_like(residual)
    search = pol_wide * residual
    rho_now = set_sums(residual, search)
    for iteration in range(ITERS):
        image_vec = operate(search)
        step_size = spread_sets(rho_now / set_sums(search, image_vec))
        dipoles = dipoles + step_size * search
        residual = residual - step_size * image_vec
        if iteration + 1 < ITERS:
            precond = pol_wide * residual
            rho_next = set_sums(residual, precond)
            search = precond + spread_sets(rho_next / rho_now) * search
            rho_now = rho_next
    return (dipoles, residual)
```

```python
import functools

import jax
import jax.numpy as jnp
from jax import lax
from jax.experimental import pallas as pl
from jax.experimental.pallas import tpu as pltpu
from jax.sharding import PartitionSpec as P

thole_factor = 0.39
column_width = 8.0
slot_moves = ((0, 1), (1, -1), (1, 0), (1, 1))
GEO_ROWS = 24
ROWS = 16
MESH = pl.DeviceIdType.MESH


def kernel(
    nx,
    ny,
    blocks,
    count_ref,
    total_ref,
    pos_ref,
    pol_ref,
    field_ref,
    list_ref,
    dip_ref,
    res_ref,
    mail,
    geo,
    vrow2,
    vhalo2,
    gmail,
    polw,
    maskw,
    resid,
    image,
    weight,
    gb,
    vb,
    fa,
    bacc,
    bown,
    tens,
    tdiag,
    toff,
    back_out,
    back_in,
    ar_out,
    arx,
    ary,
    mail_ss,
    mail_rs,
    back_ss,
    back_rs,
    arx_ss,
    arx_rs,
    ary_ss,
    ary_rs,
):
    atoms = pos_ref.shape[2]
    groups = atoms // ROWS
    comps = 6 * blocks
    vrows = polw.shape[0]
    me_x, me_y = lax.axis_index("gx"), lax.axis_index("gy")

    def device(dx, dy):
        return (lax.rem(me_x + (dx % nx), nx), lax.rem(me_y + (dy % ny), ny))

    partners = {((a * dx) % nx, (a * dy) % ny) for dx, dy in slot_moves for a in (1, -1)}
    partners |= {(d, 0) for d in range(1, nx)} | {(0, d) for d in range(1, ny)}
    partners = sorted(partners - {(0, 0)})
    barrier = pltpu.get_barrier_semaphore()
    for dx, dy in partners:
        pl.semaphore_signal(barrier, inc=1, device_id=device(dx, dy), device_id_type=MESH)

    lane = lax.broadcasted_iota(jnp.int32, (1, atoms), 1)
    mail[...] = jnp.zeros_like(mail)
    vrow2[...] = jnp.zeros_like(vrow2)
    polw[...] = jnp.ones_like(polw)
    maskw[...] = jnp.zeros_like(maskw)
    resid[...] = jnp.zeros_like(resid)
    for b in range(blocks):
        mask = (lane < count_ref[0, b]).astype(jnp.float32)
        pol = pol_ref[pl.ds(b, 1), :]
        mail[pl.ds(4 * b, 3), :] = pos_ref[b]
        mail[pl.ds(4 * b + 3, 1), :] = (thole_factor**0.5) * lax.rsqrt(pol)
        own = field_ref[b] * mask
        resid[pl.ds(6 * b, 6), :] = own
        mail[pl.ds(GEO_ROWS + 6 * b, 6), :] = own * pol
        polw[pl.ds(6 * b, 6), :] = jnp.broadcast_to(pol, (6, atoms))
        maskw[pl.ds(6 * b, 6), :] = jnp.broadcast_to(mask, (6, atoms))

    pl.semaphore_wait(barrier, len(partners))

    def send_mail(turn, source, target):
        copies = []
        for s, (dx, dy) in enumerate(slot_moves):
            copy = pltpu.make_async_remote_copy(
                src_ref=source,
                dst_ref=target.at[s],
                send_sem=mail_ss.at[turn, s],
                recv_sem=mail_rs.at[turn, s],
                device_id=device(-dx, -dy),
                device_id_type=MESH,
            )
            copy.start()
            copies.append(copy)
        return copies

    def send_back(turn):
        copies = []
        for s, (dx, dy) in enumerate(slot_moves):
            back_out[turn, s, pl.ds(0, comps), :] = jnp.sum(bacc[s], axis=1)
            copy = pltpu.make_async_remote_copy(
                src_ref=back_out.at[turn, s],
                dst_ref=back_in.at[turn, s],
                send_sem=back_ss.at[turn, s],
                recv_sem=back_rs.at[turn, s],
                device_id=device(dx, dy),
                device_id_type=MESH,
            )
            copy.start()
            copies.append(copy)
        return copies

    def spread_x(turn):
        copies = []
        for d in range(1, nx):
            copy = pltpu.make_async_remote_copy(
                src_ref=ar_out.at[turn, 0],
                dst_ref=arx.at[turn, d - 1],
                send_sem=arx_ss.at[turn, d - 1],
                recv_sem=arx_rs.at[turn, d - 1],
                device_id=device(d, 0),
                device_id_type=MESH,
            )
            copy.start()
            copies.append(copy)
        return copies

    def spread_y(turn):
        copies = []
        for d in range(1, ny):
            copy = pltpu.make_async_remote_copy(
                src_ref=ar_out.at[turn, 1],
                dst_ref=ary.at[turn, d - 1],
                send_sem=ary_ss.at[turn, d - 1],
                recv_sem=ary_rs.at[turn, d - 1],
                device_id=device(0, d),
                device_id_type=MESH,
            )
            copy.start()
            copies.append(copy)
        return copies

    started = []
    row_id = lax.broadcasted_iota(jnp.int32, (vrows, atoms), 0)
    in_set_d = lax.rem(row_id, 6) < 3

    def reduce_start(turn, products):
        parts = []
        for prod in products:
            d_part = jnp.where(in_set_d, prod, 0.0)
            parts.append(jnp.sum(d_part, axis=0, keepdims=True))
            parts.append(jnp.sum(prod - d_part, axis=0, keepdims=True))
        parts.append(jnp.zeros((8 - len(parts), atoms), jnp.float32))
        ar_out[turn, 0] = jnp.concatenate(parts, axis=0)
        copies = spread_x(turn)
        started.extend(copies)
        return copies

    def reduce_middle(turn, copies):
        total = ar_out[turn, 0]
        for d, copy in enumerate(copies):
            copy.wait_recv()
            total = total + arx[turn, d]
        ar_out[turn, 1] = total
        copies = spread_y(turn)
        started.extend(copies)
        return copies

    def reduce_end(turn, copies):
        total = ar_out[turn, 1]
        for d, copy in enumerate(copies):
            copy.wait_recv()
            total = total + ary[turn, d]
        return jnp.sum(total, axis=1, keepdims=True)

    def spread_sets(first, second):
        wide = jnp.broadcast_to(first, (vrows, atoms))
        return jnp.where(in_set_d, wide, jnp.broadcast_to(second, (vrows, atoms)))

    def broadcast_rows(rows, target, count):
        square = jnp.concatenate(
            [rows, jnp.zeros((atoms - rows.shape[0], atoms), jnp.float32)], axis=0
        ).T
        for r in range(count):
            target[r] = jnp.broadcast_to(square[:, r : r + 1], (atoms, atoms))

    def tensor(own, other, keep, diagonal):
        dx, dy, dz = other[0] - own[0], other[1] - own[1], other[2] - own[2]
        dist_sq = dx * dx + dy * dy + dz * dz
        if diagonal is not None:
            dist_sq = jnp.where(diagonal, 1.0, dist_sq)
        inv = lax.rsqrt(dist_sq)
        inv_sq = inv * inv
        damping = dist_sq * dist_sq * inv * (own[3] * other[3])
        decay = jnp.exp(-damping)
        l3 = 1.0 - decay
        l5 = l3 - damping * decay
        level = 3.0 * l5 * inv
        root = level * lax.rsqrt(level) * inv_sq
        c3 = l3 * (inv_sq * inv)
        if keep is not None:
            root = root * keep
            c3 = c3 * keep
        if diagonal is not None:
            root = jnp.where(diagonal, 0.0, root)
            c3 = jnp.where(diagonal, 0.0, c3)
        return root * dx, root * dy, root * dz, c3

    def apply(t, v):
        out = []
        for k in (0, 3):
            project = t[0] * v[k] + t[1] * v[k + 1] + t[2] * v[k + 2]
            out += [t[m] * project - t[3] * v[k + m] for m in range(3)]
        return out

    def fold(x):
        return x[0:8] + x[8:16]

    def rows_of(ref, first, count):
        return [ref[pl.ds(first + m, 1), :] for m in range(count)]

    def own_part(ref, first, g, count):
        return [ref[first + m, pl.ds(g * ROWS, ROWS), :] for m in range(count)]

    def diag_pairs(turn, vref, voff):
        def step(n, carry):
            b, g = n // groups, lax.rem(n, groups)
            if turn == 0:
                row = g * ROWS + lax.broadcasted_iota(jnp.int32, (ROWS, atoms), 0)
                col = lax.broadcasted_iota(jnp.int32, (ROWS, atoms), 1)
                t = tensor(
                    own_part(gb, 4 * b, g, 4), rows_of(mail, 4 * b, 4), None, row == col
                )
                for m in range(4):
                    tdiag[n, m] = t[m]
            else:
                t = [tdiag[n, m] for m in range(4)]
            out = apply(t, rows_of(vref, voff + 6 * b, 6))
            for m in range(6):
                fa[6 * b + m, pl.ds(g * ROWS, ROWS), :] = out[m]
            return carry

        lax.fori_loop(0, blocks * groups, step, 0)

    def off_pairs(turn, vref, voff):
        bown[...] = jnp.zeros_like(bown)

        def step(n, carry):
            b, g = n // groups, lax.rem(n, groups)
            if turn == 0:
                t = tensor(
                    own_part(gb, 4 * b, g, 4), rows_of(mail, 4 * b + 4, 4), None, None
                )
                for m in range(4):
                    toff[n, m] = t[m]
            else:
                t = [toff[n, m] for m in range(4)]
            out = apply(t, rows_of(vref, voff + 6 * b + 6, 6))
            ret = apply(t, own_part(vb, 6 * b, g, 6))
            for m in range(6):
                fa[6 * b + m, pl.ds(g * ROWS, ROWS), :] += out[m]
                bown[6 * b + 6 + m] += fold(ret[m])
            return carry

        lax.fori_loop(0, (blocks - 1) * groups, step, 0)

    def halo_pairs(turn, vhalo, voff, first, last):
        def step(n, carry):
            k, g = n // groups, lax.rem(n, groups)
            b = (k + 1) // 3
            c = k - 2 * b
            vi = own_part(vb, 6 * b, g, 6)
            if turn == 0:
                own = own_part(gb, 4 * b, g, 4)
            total = None
            for s in range(4):
                if turn == 0:
                    keep = weight[pl.ds((s + 1) * blocks * blocks + b * blocks + c, 1), :]
                    other = [geo[s, pl.ds(4 * c + m, 1), :] for m in range(4)]
                    t = tensor(own, other, keep, None)
                    for m in range(4):
                        tens[n, s, m] = t[m]
                else:
                    t = [tens[n, s, m] for m in range(4)]
                vj = [vhalo[s, pl.ds(voff + 6 * c + m, 1), :] for m in range(6)]
                out = apply(t, vj)
                total = out if total is None else [p + q for p, q in zip(total, out)]
                ret = apply(t, vi)
                for m in range(6):
                    bacc[s, 6 * c + m] += fold(ret[m])
            for m in range(6):
                fa[6 * b + m, pl.ds(g * ROWS, ROWS), :] += total[m]
            return carry

        lax.fori_loop(first * groups, last * groups, step, 0)

    lane_sq = lax.broadcasted_iota(jnp.int32, (atoms, atoms), 1)

    def own_field():
        square = jnp.zeros((atoms, atoms), jnp.float32)
        for r in range(comps):
            square = jnp.where(lane_sq == r, jnp.sum(fa[r], axis=1, keepdims=True), square)
        image[...] = jnp.zeros_like(image)
        image[pl.ds(0, comps), :] = jnp.sum(bown[...], axis=1)
        return square.T[0:vrows] + image[...]

    links = 3 * blocks - 2
    own_vec = mail.at[pl.ds(GEO_ROWS, vrows)]

    mails = send_mail(0, mail, gmail)
    started.extend(mails)
    back_out[...] = jnp.zeros_like(back_out)
    search = own_vec[...]
    first_res = resid[...]
    broadcast_rows(mail[pl.ds(0, GEO_ROWS), :], gb, 4 * blocks)
    broadcast_rows(search, vb, comps)
    entry = list_ref[...]
    code = (entry[1:2] * blocks + entry[0:1]) * blocks + entry[2:3]
    here = lax.broadcasted_iota(jnp.int32, code.shape, 1) < total_ref[0, 0]
    code = jnp.where(here, code, -1)
    names = lax.broadcasted_iota(jnp.int32, (weight.shape[0], code.shape[1]), 0)
    found = jnp.sum((names == code).astype(jnp.float32), axis=1, keepdims=True)
    weight[...] = jnp.broadcast_to(found, weight.shape)

    bacc[...] = jnp.zeros_like(bacc)
    diag_pairs(0, mail, GEO_ROWS)
    geo_row = lax.rem(lax.broadcasted_iota(jnp.int32, (GEO_ROWS, atoms), 0), 4)
    for s, (dx, dy) in enumerate(slot_moves):
        mails[s].wait_recv()
        shift = jnp.where(geo_row == 0, column_width * dx, 0.0)
        shift = jnp.where(geo_row == 1, column_width * dy, shift)
        geo[s] = gmail[s, pl.ds(0, GEO_ROWS), :] + shift
    halo_pairs(0, gmail, GEO_ROWS, 0, links)
    backs = send_back(0)
    started.extend(backs)
    off_pairs(0, mail, GEO_ROWS)
    mutual = own_field()
    for s in range(4):
        backs[s].wait_recv()
        mutual = mutual + back_in[0, s]
    image_one = search / polw[...] - mutual * maskw[...]
    vec_two = polw[...] * image_one
    vrow2[...] = vec_two

    mails = send_mail(1, vrow2, vhalo2)
    started.extend(mails)
    sums = reduce_start(0, (first_res * search, search * image_one))
    broadcast_rows(vec_two, vb, comps)
    bacc[...] = jnp.zeros_like(bacc)
    diag_pairs(1, vrow2, 0)
    for s in range(4):
        mails[s].wait_recv()
    cuts = [links * i // 5 for i in range(6)]
    halo_pairs(1, vhalo2, 0, cuts[0], cuts[1])
    sums = reduce_middle(0, sums)
    halo_pairs(1, vhalo2, 0, cuts[1], cuts[2])
    total = reduce_end(0, sums)
    rho_d, rho_p = total[0:1], total[1:2]
    step_one = spread_sets(rho_d / total[2:3], rho_p / total[3:4])
    res_one = first_res - step_one * image_one
    precond = polw[...] * res_one
    sums = reduce_start(1, (res_one * precond,))
    halo_pairs(1, vhalo2, 0, cuts[2], cuts[3])
    sums = reduce_middle(1, sums)
    halo_pairs(1, vhalo2, 0, cuts[3], cuts[5])
    backs = send_back(1)
    started.extend(backs)
    off_pairs(1, vrow2, 0)
    mutual = own_field()
    total = reduce_end(1, sums)
    next_d, next_p = total[0:1], total[1:2]
    ratio = spread_sets(next_d / rho_d, next_p / rho_p)
    for s in range(4):
        backs[s].wait_recv()
        mutual = mutual + back_in[1, s]
    image_vec = vec_two / polw[...] - mutual * maskw[...]
    search_two = precond + ratio * search
    image_two = (image_one - step_one * image_vec) + ratio * image_one
    sums = reduce_start(2, (search_two * image_two,))
    sums = reduce_middle(2, sums)
    total = reduce_end(2, sums)
    step_two = spread_sets(next_d / total[0:1], next_p / total[1:2])
    resid[...] = step_one * search + step_two * search_two
    image[...] = res_one - step_two * image_two
    for b in range(blocks):
        dip_ref[b] = resid[pl.ds(6 * b, 6), :]
        res_ref[b] = image[pl.ds(6 * b, 6), :]
    for copy in started:
        copy.wait_send()


def per_device(nx, ny, positions, polarity, direct_field, atom_count, pair_list, pair_count):
    blocks, atoms = positions.shape[2], positions.shape[4]
    groups = atoms // ROWS
    comps = 6 * blocks
    vrows = -(-comps // 8) * 8
    links = 3 * blocks - 2
    names = -(-5 * blocks * blocks // 8) * 8
    f32 = jnp.float32
    vmem = pl.BlockSpec(memory_space=pltpu.VMEM)
    smem = pl.BlockSpec(memory_space=pltpu.SMEM)
    out = jax.ShapeDtypeStruct((blocks, 6, atoms), f32)
    sem = pltpu.SemaphoreType.DMA
    dipoles, residual = pl.pallas_call(
        functools.partial(kernel, nx, ny, blocks),
        out_shape=(out, out),
        in_specs=[smem, smem, vmem, vmem, vmem, vmem],
        out_specs=(vmem, vmem),
        scratch_shapes=[
            pltpu.VMEM((GEO_ROWS + vrows, atoms), f32),
            pltpu.VMEM((4, GEO_ROWS, atoms), f32),
            pltpu.VMEM((vrows, atoms), f32),
            pltpu.VMEM((4, vrows, atoms), f32),
            pltpu.VMEM((4, GEO_ROWS + vrows, atoms), f32),
            pltpu.VMEM((vrows, atoms), f32),
            pltpu.VMEM((vrows, atoms), f32),
            pltpu.VMEM((vrows, atoms), f32),
            pltpu.VMEM((vrows, atoms), f32),
            pltpu.VMEM((names, atoms), f32),
            pltpu.VMEM((4 * blocks, atoms, atoms), f32),
            pltpu.VMEM((comps, atoms, atoms), f32),
            pltpu.VMEM((comps, atoms, atoms), f32),
            pltpu.VMEM((4, comps, 8, atoms), f32),
            pltpu.VMEM((comps, 8, atoms), f32),
            pltpu.VMEM((links * groups, 4, 4, ROWS, atoms), f32),
            pltpu.VMEM((blocks * groups, 4, ROWS, atoms), f32),
            pltpu.VMEM(((blocks - 1) * groups, 4, ROWS, atoms), f32),
            pltpu.VMEM((2, 4, vrows, atoms), f32),
            pltpu.VMEM((2, 4, vrows, atoms), f32),
            pltpu.VMEM((3, 2, 8, atoms), f32),
            pltpu.VMEM((3, nx - 1, 8, atoms), f32),
            pltpu.VMEM((3, ny - 1, 8, atoms), f32),
            sem((2, 4)),
            sem((2, 4)),
            sem((2, 4)),
            sem((2, 4)),
            sem((3, nx - 1)),
            sem((3, nx - 1)),
            sem((3, ny - 1)),
            sem((3, ny - 1)),
        ],
        compiler_params=pltpu.CompilerParams(
            collective_id=0, has_side_effects=True, vmem_limit_bytes=40 * 1024 * 1024
        ),
    )(
        atom_count[0],
        pair_count,
        positions[0, 0],
        polarity[0, 0],
        direct_field[0, 0],
        pair_list[0, 0],
    )
    return (dipoles[None, None], residual[None, None])


def solution(mesh):
    in_specs = (
        P("gx", "gy", None, None, None),
        P("gx", "gy", None, None),
        P("gx", "gy", None, None, None),
        P("gx", "gy", None),
        P("gx", "gy", None, None),
        P("gx", "gy"),
    )
    out_specs = (P("gx", "gy", None, None, None), P("gx", "gy", None, None, None))
    body = functools.partial(per_device, mesh.shape["gx"], mesh.shape["gy"])
    return jax.shard_map(
        body, mesh=mesh, in_specs=in_specs, out_specs=out_specs, check_vma=False
    )
```

```python
import functools

import jax
import jax.numpy as jnp
from jax import lax
from jax.experimental import pallas as pl
from jax.experimental.pallas import tpu as pltpu
from jax.sharding import PartitionSpec as P

thole_factor = 0.39
column_width = 8.0
slot_moves = ((0, 1), (1, -1), (1, 0), (1, 1))
GEO_ROWS = 24
ROWS = 16
slot_order = (2, 0, 1, 3)
MESH = pl.DeviceIdType.MESH


def kernel(
    nx,
    ny,
    blocks,
    count_ref,
    total_ref,
    pos_ref,
    pol_ref,
    field_ref,
    list_ref,
    dip_ref,
    res_ref,
    mail,
    geo,
    vrow2,
    vhalo2,
    gmail,
    polw,
    maskw,
    resid,
    image,
    weight,
    gb,
    vb,
    fa,
    bacc,
    bown,
    tens,
    tdiag,
    toff,
    back_out,
    back_in,
    ar_out,
    arx,
    ary,
    mail_ss,
    mail_rs,
    back_ss,
    back_rs,
    arx_ss,
    arx_rs,
    ary_ss,
    ary_rs,
):
    atoms = pos_ref.shape[2]
    groups = atoms // ROWS
    links = 3 * blocks - 2
    comps = 6 * blocks
    vrows = polw.shape[0]
    me_x, me_y = lax.axis_index("gx"), lax.axis_index("gy")

    def device(dx, dy):
        return (lax.rem(me_x + (dx % nx), nx), lax.rem(me_y + (dy % ny), ny))

    partners = {((a * dx) % nx, (a * dy) % ny) for dx, dy in slot_moves for a in (1, -1)}
    partners |= {(d, 0) for d in range(1, nx)} | {(0, d) for d in range(1, ny)}
    partners = sorted(partners - {(0, 0)})
    barrier = pltpu.get_barrier_semaphore()
    for dx, dy in partners:
        pl.semaphore_signal(barrier, inc=1, device_id=device(dx, dy), device_id_type=MESH)

    lane = lax.broadcasted_iota(jnp.int32, (1, atoms), 1)
    mail[...] = jnp.zeros_like(mail)
    vrow2[...] = jnp.zeros_like(vrow2)
    polw[...] = jnp.ones_like(polw)
    maskw[...] = jnp.zeros_like(maskw)
    resid[...] = jnp.zeros_like(resid)
    for b in range(blocks):
        mask = (lane < count_ref[0, b]).astype(jnp.float32)
        pol = pol_ref[pl.ds(b, 1), :]
        mail[pl.ds(4 * b, 3), :] = pos_ref[b]
        mail[pl.ds(4 * b + 3, 1), :] = (thole_factor**0.5) * lax.rsqrt(pol)
        own = field_ref[b] * mask
        resid[pl.ds(6 * b, 6), :] = own
        mail[pl.ds(GEO_ROWS + 6 * b, 6), :] = own * pol
        polw[pl.ds(6 * b, 6), :] = jnp.broadcast_to(pol, (6, atoms))
        maskw[pl.ds(6 * b, 6), :] = jnp.broadcast_to(mask, (6, atoms))

    started = []

    def send_mail(turn, source, target):
        copies = {}
        for s in slot_order:
            dx, dy = slot_moves[s]
            copy = pltpu.make_async_remote_copy(
                src_ref=source,
                dst_ref=target.at[s],
                send_sem=mail_ss.at[turn, s],
                recv_sem=mail_rs.at[turn, s],
                device_id=device(-dx, -dy),
                device_id_type=MESH,
            )
            copy.start()
            started.append(copy)
            copies[s] = copy
        return copies

    def send_back(turn, s):
        back_out[turn, s, pl.ds(0, comps), :] = jnp.sum(bacc[s], axis=1)
        copy = pltpu.make_async_remote_copy(
            src_ref=back_out.at[turn, s],
            dst_ref=back_in.at[turn, s],
            send_sem=back_ss.at[turn, s],
            recv_sem=back_rs.at[turn, s],
            device_id=device(*slot_moves[s]),
            device_id_type=MESH,
        )
        copy.start()
        started.append(copy)
        return copy

    def spread_x(turn):
        copies = []
        for d in range(1, nx):
            copy = pltpu.make_async_remote_copy(
                src_ref=ar_out.at[turn, 0],
                dst_ref=arx.at[turn, d - 1],
                send_sem=arx_ss.at[turn, d - 1],
                recv_sem=arx_rs.at[turn, d - 1],
                device_id=device(d, 0),
                device_id_type=MESH,
            )
            copy.start()
            copies.append(copy)
        return copies

    def spread_y(turn):
        copies = []
        for d in range(1, ny):
            copy = pltpu.make_async_remote_copy(
                src_ref=ar_out.at[turn, 1],
                dst_ref=ary.at[turn, d - 1],
                send_sem=ary_ss.at[turn, d - 1],
                recv_sem=ary_rs.at[turn, d - 1],
                device_id=device(0, d),
                device_id_type=MESH,
            )
            copy.start()
            copies.append(copy)
        return copies

    row_id = lax.broadcasted_iota(jnp.int32, (vrows, atoms), 0)
    in_set_d = lax.rem(row_id, 6) < 3

    def reduce_start(turn, products):
        parts = []
        for prod in products:
            d_part = jnp.where(in_set_d, prod, 0.0)
            parts.append(jnp.sum(d_part, axis=0, keepdims=True))
            parts.append(jnp.sum(prod - d_part, axis=0, keepdims=True))
        parts.append(jnp.zeros((8 - len(parts), atoms), jnp.float32))
        ar_out[turn, 0] = jnp.concatenate(parts, axis=0)
        copies = spread_x(turn)
        started.extend(copies)
        return copies

    def reduce_middle(turn, copies):
        total = ar_out[turn, 0]
        for d, copy in enumerate(copies):
            copy.wait_recv()
            total = total + arx[turn, d]
        ar_out[turn, 1] = total
        copies = spread_y(turn)
        started.extend(copies)
        return copies

    def reduce_end(turn, copies):
        total = ar_out[turn, 1]
        for d, copy in enumerate(copies):
            copy.wait_recv()
            total = total + ary[turn, d]
        return jnp.sum(total, axis=1, keepdims=True)

    def spread_sets(first, second):
        wide = jnp.broadcast_to(first, (vrows, atoms))
        return jnp.where(in_set_d, wide, jnp.broadcast_to(second, (vrows, atoms)))

    def broadcast_rows(rows, target, count):
        square = jnp.concatenate(
            [rows, jnp.zeros((atoms - rows.shape[0], atoms), jnp.float32)], axis=0
        ).T
        for r in range(count):
            target[r] = jnp.broadcast_to(square[:, r : r + 1], (atoms, atoms))

    def tensor(own, other, keep, diagonal):
        dx, dy, dz = other[0] - own[0], other[1] - own[1], other[2] - own[2]
        dist_sq = dx * dx + dy * dy + dz * dz
        if diagonal is not None:
            dist_sq = jnp.where(diagonal, 1.0, dist_sq)
        inv = lax.rsqrt(dist_sq)
        inv_sq = inv * inv
        damping = dist_sq * dist_sq * inv * (own[3] * other[3])
        decay = jnp.exp(-damping)
        l3 = 1.0 - decay
        l5 = l3 - damping * decay
        level = 3.0 * l5 * inv
        root = level * lax.rsqrt(level) * inv_sq
        c3 = l3 * (inv_sq * inv)
        if keep is not None:
            root = root * keep
            c3 = c3 * keep
        if diagonal is not None:
            root = jnp.where(diagonal, 0.0, root)
            c3 = jnp.where(diagonal, 0.0, c3)
        return root * dx, root * dy, root * dz, c3

    def apply(t, v):
        out = []
        for k in (0, 3):
            project = t[0] * v[k] + t[1] * v[k + 1] + t[2] * v[k + 2]
            out += [t[m] * project - t[3] * v[k + m] for m in range(3)]
        return out

    def fold(x):
        return x[0:8] + x[8:16]

    def rows_of(ref, first, count):
        return [ref[pl.ds(first + m, 1), :] for m in range(count)]

    def own_part(ref, first, g, count):
        return [ref[first + m, pl.ds(g * ROWS, ROWS), :] for m in range(count)]

    def diag_pairs(turn, vref, voff):
        def step(n, carry):
            b, g = n // groups, lax.rem(n, groups)
            if turn == 0:
                row = g * ROWS + lax.broadcasted_iota(jnp.int32, (ROWS, atoms), 0)
                col = lax.broadcasted_iota(jnp.int32, (ROWS, atoms), 1)
                t = tensor(
                    own_part(gb, 4 * b, g, 4), rows_of(mail, 4 * b, 4), None, row == col
                )
                for m in range(4):
                    tdiag[n, m] = t[m]
            else:
                t = [tdiag[n, m] for m in range(4)]
            out = apply(t, rows_of(vref, voff + 6 * b, 6))
            for m in range(6):
                fa[6 * b + m, pl.ds(g * ROWS, ROWS), :] = out[m]
            return carry

        lax.fori_loop(0, blocks * groups, step, 0)

    def off_pairs(turn, vref, voff):
        bown[...] = jnp.zeros_like(bown)

        def step(n, carry):
            b, g = n // groups, lax.rem(n, groups)
            if turn == 0:
                t = tensor(
                    own_part(gb, 4 * b, g, 4), rows_of(mail, 4 * b + 4, 4), None, None
                )
                for m in range(4):
                    toff[n, m] = t[m]
            else:
                t = [toff[n, m] for m in range(4)]
            out = apply(t, rows_of(vref, voff + 6 * b + 6, 6))
            ret = apply(t, own_part(vb, 6 * b, g, 6))
            for m in range(6):
                fa[6 * b + m, pl.ds(g * ROWS, ROWS), :] += out[m]
                bown[6 * b + 6 + m] += fold(ret[m])
            return carry

        lax.fori_loop(0, (blocks - 1) * groups, step, 0)

    def halo_pairs(turn, s, vhalo, voff):
        chunk = 2 if groups % 2 == 0 else 1

        def step(n, carry):
            k, part = n // (groups // chunk), lax.rem(n, groups // chunk)
            b = (k + 1) // 3
            c = k - 2 * b
            vj = [vhalo[s, pl.ds(voff + 6 * c + m, 1), :] for m in range(6)]
            if turn == 0:
                keep = weight[pl.ds((s + 1) * blocks * blocks + b * blocks + c, 1), :]
                other = [geo[s, pl.ds(4 * c + m, 1), :] for m in range(4)]
            back = None
            for h in range(chunk):
                g = part * chunk + h
                at = k * groups + g
                if turn == 0:
                    t = tensor(own_part(gb, 4 * b, g, 4), other, keep, None)
                    for m in range(4):
                        tens[at, s, m] = t[m]
                else:
                    t = [tens[at, s, m] for m in range(4)]
                out = apply(t, vj)
                for m in range(6):
                    fa[6 * b + m, pl.ds(g * ROWS, ROWS), :] += out[m]
                ret = [fold(r) for r in apply(t, own_part(vb, 6 * b, g, 6))]
                back = ret if back is None else [p + q for p, q in zip(back, ret)]
            for m in range(6):
                bacc[s, 6 * c + m] += back[m]
            return carry

        lax.fori_loop(0, links * (groups // chunk), step, 0)

    lane_sq = lax.broadcasted_iota(jnp.int32, (atoms, atoms), 1)

    def own_field():
        square = jnp.zeros((atoms, atoms), jnp.float32)
        for r in range(comps):
            square = jnp.where(lane_sq == r, jnp.sum(fa[r], axis=1, keepdims=True), square)
        image[...] = jnp.zeros_like(image)
        image[pl.ds(0, comps), :] = jnp.sum(bown[...], axis=1)
        return square.T[0:vrows] + image[...]

    own_vec = mail.at[pl.ds(GEO_ROWS, vrows)]

    back_out[...] = jnp.zeros_like(back_out)
    bacc[...] = jnp.zeros_like(bacc)
    search = own_vec[...]
    first_res = resid[...]
    broadcast_rows(mail[pl.ds(0, GEO_ROWS), :], gb, 4 * blocks)
    broadcast_rows(search, vb, comps)
    entry = list_ref[...]
    code = (entry[1:2] * blocks + entry[0:1]) * blocks + entry[2:3]
    here = lax.broadcasted_iota(jnp.int32, code.shape, 1) < total_ref[0, 0]
    code = jnp.where(here, code, -1)
    names = lax.broadcasted_iota(jnp.int32, (weight.shape[0], code.shape[1]), 0)
    found = jnp.sum((names == code).astype(jnp.float32), axis=1, keepdims=True)
    weight[...] = jnp.broadcast_to(found, weight.shape)

    pl.semaphore_wait(barrier, len(partners))
    mails = send_mail(0, mail, gmail)
    diag_pairs(0, mail, GEO_ROWS)
    geo_row = lax.rem(lax.broadcasted_iota(jnp.int32, (GEO_ROWS, atoms), 0), 4)
    backs = {}
    for s in slot_order:
        dx, dy = slot_moves[s]
        mails[s].wait_recv()
        shift = jnp.where(geo_row == 0, column_width * dx, 0.0)
        shift = jnp.where(geo_row == 1, column_width * dy, shift)
        geo[s] = gmail[s, pl.ds(0, GEO_ROWS), :] + shift
        halo_pairs(0, s, gmail, GEO_ROWS)
        backs[s] = send_back(0, s)
    off_pairs(0, mail, GEO_ROWS)
    mutual = own_field()
    for s in slot_order:
        backs[s].wait_recv()
        mutual = mutual + back_in[0, s]
    image_one = search / polw[...] - mutual * maskw[...]
    vec_two = polw[...] * image_one
    vrow2[...] = vec_two

    mails = send_mail(1, vrow2, vhalo2)
    sums = reduce_start(0, (first_res * search, search * image_one))
    broadcast_rows(vec_two, vb, comps)
    bacc[...] = jnp.zeros_like(bacc)
    diag_pairs(1, vrow2, 0)
    for place, s in enumerate(slot_order):
        mails[s].wait_recv()
        halo_pairs(1, s, vhalo2, 0)
        backs[s] = send_back(1, s)
        if place == 0:
            sums = reduce_middle(0, sums)
        elif place == 1:
            total = reduce_end(0, sums)
            rho_d, rho_p = total[0:1], total[1:2]
            step_one = spread_sets(rho_d / total[2:3], rho_p / total[3:4])
            res_one = first_res - step_one * image_one
            precond = polw[...] * res_one
            sums = reduce_start(1, (res_one * precond,))
        elif place == 2:
            sums = reduce_middle(1, sums)
    off_pairs(1, vrow2, 0)
    mutual = own_field()
    total = reduce_end(1, sums)
    next_d, next_p = total[0:1], total[1:2]
    ratio = spread_sets(next_d / rho_d, next_p / rho_p)
    search_two = precond + ratio * search
    own_image = vec_two / polw[...]
    product = search_two * mutual
    for s in range(4):
        start = gmail[s, pl.ds(GEO_ROWS, vrows), :]
        halo_two = (start - step_one * vhalo2[s]) + ratio * start
        product = product + halo_two * back_out[1, s]
    product = step_one * product + search_two * (
        (image_one - step_one * own_image) + ratio * image_one
    )
    sums = reduce_start(2, (product,))
    sums = reduce_middle(2, sums)
    for s in slot_order:
        backs[s].wait_recv()
        mutual = mutual + back_in[1, s]
    image_vec = own_image - mutual * maskw[...]
    image_two = (image_one - step_one * image_vec) + ratio * image_one
    total = reduce_end(2, sums)
    step_two = spread_sets(next_d / total[0:1], next_p / total[1:2])
    resid[...] = step_one * search + step_two * search_two
    image[...] = res_one - step_two * image_two
    for b in range(blocks):
        dip_ref[b] = resid[pl.ds(6 * b, 6), :]
        res_ref[b] = image[pl.ds(6 * b, 6), :]
    for copy in started:
        copy.wait_send()


def per_device(nx, ny, positions, polarity, direct_field, atom_count, pair_list, pair_count):
    blocks, atoms = positions.shape[2], positions.shape[4]
    groups = atoms // ROWS
    comps = 6 * blocks
    vrows = -(-comps // 8) * 8
    links = 3 * blocks - 2
    names = -(-5 * blocks * blocks // 8) * 8
    f32 = jnp.float32
    vmem = pl.BlockSpec(memory_space=pltpu.VMEM)
    smem = pl.BlockSpec(memory_space=pltpu.SMEM)
    out = jax.ShapeDtypeStruct((blocks, 6, atoms), f32)
    sem = pltpu.SemaphoreType.DMA
    dipoles, residual = pl.pallas_call(
        functools.partial(kernel, nx, ny, blocks),
        out_shape=(out, out),
        in_specs=[smem, smem, vmem, vmem, vmem, vmem],
        out_specs=(vmem, vmem),
        scratch_shapes=[
            pltpu.VMEM((GEO_ROWS + vrows, atoms), f32),
            pltpu.VMEM((4, GEO_ROWS, atoms), f32),
            pltpu.VMEM((vrows, atoms), f32),
            pltpu.VMEM((4, vrows, atoms), f32),
            pltpu.VMEM((4, GEO_ROWS + vrows, atoms), f32),
            pltpu.VMEM((vrows, atoms), f32),
            pltpu.VMEM((vrows, atoms), f32),
            pltpu.VMEM((vrows, atoms), f32),
            pltpu.VMEM((vrows, atoms), f32),
            pltpu.VMEM((names, atoms), f32),
            pltpu.VMEM((4 * blocks, atoms, atoms), f32),
            pltpu.VMEM((comps, atoms, atoms), f32),
            pltpu.VMEM((comps, atoms, atoms), f32),
            pltpu.VMEM((4, comps, 8, atoms), f32),
            pltpu.VMEM((comps, 8, atoms), f32),
            pltpu.VMEM((links * groups, 4, 4, ROWS, atoms), f32),
            pltpu.VMEM((blocks * groups, 4, ROWS, atoms), f32),
            pltpu.VMEM(((blocks - 1) * groups, 4, ROWS, atoms), f32),
            pltpu.VMEM((2, 4, vrows, atoms), f32),
            pltpu.VMEM((2, 4, vrows, atoms), f32),
            pltpu.VMEM((3, 2, 8, atoms), f32),
            pltpu.VMEM((3, nx - 1, 8, atoms), f32),
            pltpu.VMEM((3, ny - 1, 8, atoms), f32),
            sem((2, 4)),
            sem((2, 4)),
            sem((2, 4)),
            sem((2, 4)),
            sem((3, nx - 1)),
            sem((3, nx - 1)),
            sem((3, ny - 1)),
            sem((3, ny - 1)),
        ],
        compiler_params=pltpu.CompilerParams(
            collective_id=0, has_side_effects=True, vmem_limit_bytes=40 * 1024 * 1024
        ),
    )(
        atom_count[0],
        pair_count,
        positions[0, 0],
        polarity[0, 0],
        direct_field[0, 0],
        pair_list[0, 0],
    )
    return (dipoles[None, None], residual[None, None])


def solution(mesh):
    in_specs = (
        P("gx", "gy", None, None, None),
        P("gx", "gy", None, None),
        P("gx", "gy", None, None, None),
        P("gx", "gy", None),
        P("gx", "gy", None, None),
        P("gx", "gy"),
    )
    out_specs = (P("gx", "gy", None, None, None), P("gx", "gy", None, None, None))
    body = functools.partial(per_device, mesh.shape["gx"], mesh.shape["gy"])
    return jax.shard_map(
        body, mesh=mesh, in_specs=in_specs, out_specs=out_specs, check_vma=False
    )
```

```python
import functools

import jax
import jax.numpy as jnp
from jax import lax
from jax.experimental import pallas as pl
from jax.experimental.pallas import tpu as pltpu
from jax.sharding import PartitionSpec as P

thole_factor = 0.39
column_width = 8.0
slot_moves = ((0, 1), (1, -1), (1, 0), (1, 1))
GEO_ROWS = 24
ROWS = 32
slot_order = (2, 0, 1, 3)
MESH = pl.DeviceIdType.MESH


def kernel(
    nx,
    ny,
    blocks,
    count_ref,
    total_ref,
    pos_ref,
    pol_ref,
    field_ref,
    list_ref,
    dip_ref,
    res_ref,
    mail,
    geo,
    vrow2,
    vhalo2,
    gmail,
    polw,
    maskw,
    resid,
    image,
    weight,
    gb,
    vb,
    fa,
    bacc,
    bown,
    tens,
    tdiag,
    toff,
    back_out,
    back_in,
    ar_out,
    arx,
    ary,
    mail_ss,
    mail_rs,
    back_ss,
    back_rs,
    arx_ss,
    arx_rs,
    ary_ss,
    ary_rs,
):
    atoms = pos_ref.shape[2]
    groups = atoms // ROWS
    links = 3 * blocks - 2
    comps = 6 * blocks
    vrows = polw.shape[0]
    me_x, me_y = lax.axis_index("gx"), lax.axis_index("gy")

    def device(dx, dy):
        return (lax.rem(me_x + (dx % nx), nx), lax.rem(me_y + (dy % ny), ny))

    partners = {((a * dx) % nx, (a * dy) % ny) for dx, dy in slot_moves for a in (1, -1)}
    partners |= {(d, 0) for d in range(1, nx)} | {(0, d) for d in range(1, ny)}
    partners = sorted(partners - {(0, 0)})
    barrier = pltpu.get_barrier_semaphore()
    for dx, dy in partners:
        pl.semaphore_signal(barrier, inc=1, device_id=device(dx, dy), device_id_type=MESH)

    lane = lax.broadcasted_iota(jnp.int32, (1, atoms), 1)
    mail[...] = jnp.zeros_like(mail)
    vrow2[...] = jnp.zeros_like(vrow2)
    polw[...] = jnp.ones_like(polw)
    maskw[...] = jnp.zeros_like(maskw)
    resid[...] = jnp.zeros_like(resid)
    for b in range(blocks):
        mask = (lane < count_ref[0, b]).astype(jnp.float32)
        pol = pol_ref[pl.ds(b, 1), :]
        mail[pl.ds(4 * b, 3), :] = pos_ref[b]
        mail[pl.ds(4 * b + 3, 1), :] = (thole_factor**0.5) * lax.rsqrt(pol)
        own = field_ref[b] * mask
        resid[pl.ds(6 * b, 6), :] = own
        mail[pl.ds(GEO_ROWS + 6 * b, 6), :] = own * pol
        polw[pl.ds(6 * b, 6), :] = jnp.broadcast_to(pol, (6, atoms))
        maskw[pl.ds(6 * b, 6), :] = jnp.broadcast_to(mask, (6, atoms))

    started = []

    def send_mail(turn, source, target):
        copies = {}
        for s in slot_order:
            dx, dy = slot_moves[s]
            copy = pltpu.make_async_remote_copy(
                src_ref=source,
                dst_ref=target.at[s],
                send_sem=mail_ss.at[turn, s],
                recv_sem=mail_rs.at[turn, s],
                device_id=device(-dx, -dy),
                device_id_type=MESH,
            )
            copy.start()
            started.append(copy)
            copies[s] = copy
        return copies

    def send_back(turn, s):
        back_out[turn, s, pl.ds(0, comps), :] = jnp.sum(bacc[s], axis=1)
        copy = pltpu.make_async_remote_copy(
            src_ref=back_out.at[turn, s],
            dst_ref=back_in.at[turn, s],
            send_sem=back_ss.at[turn, s],
            recv_sem=back_rs.at[turn, s],
            device_id=device(*slot_moves[s]),
            device_id_type=MESH,
        )
        copy.start()
        started.append(copy)
        return copy

    def spread_x(turn):
        copies = []
        for d in range(1, nx):
            copy = pltpu.make_async_remote_copy(
                src_ref=ar_out.at[turn, 0],
                dst_ref=arx.at[turn, d - 1],
                send_sem=arx_ss.at[turn, d - 1],
                recv_sem=arx_rs.at[turn, d - 1],
                device_id=device(d, 0),
                device_id_type=MESH,
            )
            copy.start()
            copies.append(copy)
        return copies

    def spread_y(turn):
        copies = []
        for d in range(1, ny):
            copy = pltpu.make_async_remote_copy(
                src_ref=ar_out.at[turn, 1],
                dst_ref=ary.at[turn, d - 1],
                send_sem=ary_ss.at[turn, d - 1],
                recv_sem=ary_rs.at[turn, d - 1],
                device_id=device(0, d),
                device_id_type=MESH,
            )
            copy.start()
            copies.append(copy)
        return copies

    row_id = lax.broadcasted_iota(jnp.int32, (vrows, atoms), 0)
    in_set_d = lax.rem(row_id, 6) < 3

    def reduce_start(turn, products):
        parts = []
        for prod in products:
            d_part = jnp.where(in_set_d, prod, 0.0)
            parts.append(jnp.sum(d_part, axis=0, keepdims=True))
            parts.append(jnp.sum(prod - d_part, axis=0, keepdims=True))
        parts.append(jnp.zeros((8 - len(parts), atoms), jnp.float32))
        ar_out[turn, 0] = jnp.concatenate(parts, axis=0)
        copies = spread_x(turn)
        started.extend(copies)
        return copies

    def reduce_middle(turn, copies):
        total = ar_out[turn, 0]
        for d, copy in enumerate(copies):
            copy.wait_recv()
            total = total + arx[turn, d]
        ar_out[turn, 1] = total
        copies = spread_y(turn)
        started.extend(copies)
        return copies

    def reduce_end(turn, copies):
        total = ar_out[turn, 1]
        for d, copy in enumerate(copies):
            copy.wait_recv()
            total = total + ary[turn, d]
        return jnp.sum(total, axis=1, keepdims=True)

    def spread_sets(first, second):
        wide = jnp.broadcast_to(first, (vrows, atoms))
        return jnp.where(in_set_d, wide, jnp.broadcast_to(second, (vrows, atoms)))

    def broadcast_rows(rows, target, count):
        square = jnp.concatenate(
            [rows, jnp.zeros((atoms - rows.shape[0], atoms), jnp.float32)], axis=0
        ).T
        for r in range(count):
            target[r] = jnp.broadcast_to(square[:, r : r + 1], (atoms, atoms))

    def tensor(own, other, keep, diagonal):
        dx, dy, dz = other[0] - own[0], other[1] - own[1], other[2] - own[2]
        dist_sq = dx * dx + dy * dy + dz * dz
        if diagonal is not None:
            dist_sq = jnp.where(diagonal, 1.0, dist_sq)
        inv = lax.rsqrt(dist_sq)
        inv_sq = inv * inv
        damping = dist_sq * dist_sq * inv * (own[3] * other[3])
        decay = jnp.exp(-damping)
        l3 = 1.0 - decay
        l5 = l3 - damping * decay
        level = 3.0 * l5 * inv
        root = level * lax.rsqrt(level) * inv_sq
        c3 = l3 * (inv_sq * inv)
        if keep is not None:
            root = root * keep
            c3 = c3 * keep
        if diagonal is not None:
            root = jnp.where(diagonal, 0.0, root)
            c3 = jnp.where(diagonal, 0.0, c3)
        return root * dx, root * dy, root * dz, c3

    def apply(t, v):
        out = []
        for k in (0, 3):
            project = t[0] * v[k] + t[1] * v[k + 1] + t[2] * v[k + 2]
            out += [t[m] * project - t[3] * v[k + m] for m in range(3)]
        return out

    def fold(x):
        return jnp.sum(x.reshape(ROWS // 8, 8, atoms), axis=0)

    def rows_of(ref, first, count):
        return [ref[pl.ds(first + m, 1), :] for m in range(count)]

    def own_part(ref, first, g, count):
        return [ref[first + m, pl.ds(g * ROWS, ROWS), :] for m in range(count)]

    def diag_pairs(turn, vref, voff):
        def step(n, carry):
            b, g = n // groups, lax.rem(n, groups)
            if turn == 0:
                row = g * ROWS + lax.broadcasted_iota(jnp.int32, (ROWS, atoms), 0)
                col = lax.broadcasted_iota(jnp.int32, (ROWS, atoms), 1)
                t = tensor(
                    own_part(gb, 4 * b, g, 4), rows_of(mail, 4 * b, 4), None, row == col
                )
                for m in range(4):
                    tdiag[n, m] = t[m]
            else:
                t = [tdiag[n, m] for m in range(4)]
            out = apply(t, rows_of(vref, voff + 6 * b, 6))
            for m in range(6):
                fa[6 * b + m, pl.ds(g * ROWS, ROWS), :] = out[m]
            return carry

        lax.fori_loop(0, blocks * groups, step, 0)

    def off_pairs(turn, vref, voff):
        bown[...] = jnp.zeros_like(bown)

        def step(n, carry):
            b, g = n // groups, lax.rem(n, groups)
            if turn == 0:
                t = tensor(
                    own_part(gb, 4 * b, g, 4), rows_of(mail, 4 * b + 4, 4), None, None
                )
                for m in range(4):
                    toff[n, m] = t[m]
            else:
                t = [toff[n, m] for m in range(4)]
            out = apply(t, rows_of(vref, voff + 6 * b + 6, 6))
            ret = apply(t, own_part(vb, 6 * b, g, 6))
            for m in range(6):
                fa[6 * b + m, pl.ds(g * ROWS, ROWS), :] += out[m]
                bown[6 * b + 6 + m] += fold(ret[m])
            return carry

        lax.fori_loop(0, (blocks - 1) * groups, step, 0)

    def halo_pairs(turn, s, vhalo, voff):
        chunk = 4 if groups % 4 == 0 else 1

        def step(n, carry):
            k, part = n // (groups // chunk), lax.rem(n, groups // chunk)
            b = (k + 1) // 3
            c = k - 2 * b
            vj = [vhalo[s, pl.ds(voff + 6 * c + m, 1), :] for m in range(6)]
            if turn == 0:
                keep = weight[pl.ds((s + 1) * blocks * blocks + b * blocks + c, 1), :]
                other = [geo[s, pl.ds(4 * c + m, 1), :] for m in range(4)]
            back = None
            for h in range(chunk):
                g = part * chunk + h
                at = k * groups + g
                if turn == 0:
                    t = tensor(own_part(gb, 4 * b, g, 4), other, keep, None)
                    for m in range(4):
                        tens[at, s, m] = t[m]
                else:
                    t = [tens[at, s, m] for m in range(4)]
                out = apply(t, vj)
                for m in range(6):
                    fa[6 * b + m, pl.ds(g * ROWS, ROWS), :] += out[m]
                ret = [fold(r) for r in apply(t, own_part(vb, 6 * b, g, 6))]
                back = ret if back is None else [p + q for p, q in zip(back, ret)]
            for m in range(6):
                bacc[s, 6 * c + m] += back[m]
            return carry

        lax.fori_loop(0, links * (groups // chunk), step, 0)

    lane_sq = lax.broadcasted_iota(jnp.int32, (atoms, atoms), 1)

    def own_field():
        square = jnp.zeros((atoms, atoms), jnp.float32)
        for r in range(comps):
            square = jnp.where(lane_sq == r, jnp.sum(fa[r], axis=1, keepdims=True), square)
        image[...] = jnp.zeros_like(image)
        image[pl.ds(0, comps), :] = jnp.sum(bown[...], axis=1)
        return square.T[0:vrows] + image[...]

    own_vec = mail.at[pl.ds(GEO_ROWS, vrows)]

    back_out[...] = jnp.zeros_like(back_out)
    bacc[...] = jnp.zeros_like(bacc)
    search = own_vec[...]
    first_res = resid[...]
    broadcast_rows(mail[pl.ds(0, GEO_ROWS), :], gb, 4 * blocks)
    broadcast_rows(search, vb, comps)
    entry = list_ref[...]
    code = (entry[1:2] * blocks + entry[0:1]) * blocks + entry[2:3]
    here = lax.broadcasted_iota(jnp.int32, code.shape, 1) < total_ref[0, 0]
    code = jnp.where(here, code, -1)
    names = lax.broadcasted_iota(jnp.int32, (weight.shape[0], code.shape[1]), 0)
    found = jnp.sum((names == code).astype(jnp.float32), axis=1, keepdims=True)
    weight[...] = jnp.broadcast_to(found, weight.shape)

    pl.semaphore_wait(barrier, len(partners))
    mails = send_mail(0, mail, gmail)
    diag_pairs(0, mail, GEO_ROWS)
    geo_row = lax.rem(lax.broadcasted_iota(jnp.int32, (GEO_ROWS, atoms), 0), 4)
    backs = {}
    for s in slot_order:
        dx, dy = slot_moves[s]
        mails[s].wait_recv()
        shift = jnp.where(geo_row == 0, column_width * dx, 0.0)
        shift = jnp.where(geo_row == 1, column_width * dy, shift)
        geo[s] = gmail[s, pl.ds(0, GEO_ROWS), :] + shift
        halo_pairs(0, s, gmail, GEO_ROWS)
        backs[s] = send_back(0, s)
    off_pairs(0, mail, GEO_ROWS)
    mutual = own_field()
    for s in slot_order:
        backs[s].wait_recv()
        mutual = mutual + back_in[0, s]
    image_one = search / polw[...] - mutual * maskw[...]
    vec_two = polw[...] * image_one
    vrow2[...] = vec_two

    mails = send_mail(1, vrow2, vhalo2)
    sums = reduce_start(0, (first_res * search, search * image_one))
    broadcast_rows(vec_two, vb, comps)
    bacc[...] = jnp.zeros_like(bacc)
    diag_pairs(1, vrow2, 0)
    for place, s in enumerate(slot_order):
        mails[s].wait_recv()
        halo_pairs(1, s, vhalo2, 0)
        backs[s] = send_back(1, s)
        if place == 0:
            sums = reduce_middle(0, sums)
        elif place == 1:
            total = reduce_end(0, sums)
            rho_d, rho_p = total[0:1], total[1:2]
            step_one = spread_sets(rho_d / total[2:3], rho_p / total[3:4])
            res_one = first_res - step_one * image_one
            precond = polw[...] * res_one
            sums = reduce_start(1, (res_one * precond,))
        elif place == 2:
            sums = reduce_middle(1, sums)
    off_pairs(1, vrow2, 0)
    mutual = own_field()
    total = reduce_end(1, sums)
    next_d, next_p = total[0:1], total[1:2]
    ratio = spread_sets(next_d / rho_d, next_p / rho_p)
    search_two = precond + ratio * search
    own_image = vec_two / polw[...]
    product = search_two * mutual
    for s in range(4):
        start = gmail[s, pl.ds(GEO_ROWS, vrows), :]
        halo_two = (start - step_one * vhalo2[s]) + ratio * start
        product = product + halo_two * back_out[1, s]
    product = step_one * product + search_two * (
        (image_one - step_one * own_image) + ratio * image_one
    )
    sums = reduce_start(2, (product,))
    sums = reduce_middle(2, sums)
    for s in slot_order:
        backs[s].wait_recv()
        mutual = mutual + back_in[1, s]
    image_vec = own_image - mutual * maskw[...]
    image_two = (image_one - step_one * image_vec) + ratio * image_one
    total = reduce_end(2, sums)
    step_two = spread_sets(next_d / total[0:1], next_p / total[1:2])
    resid[...] = step_one * search + step_two * search_two
    image[...] = res_one - step_two * image_two
    for b in range(blocks):
        dip_ref[b] = resid[pl.ds(6 * b, 6), :]
        res_ref[b] = image[pl.ds(6 * b, 6), :]
    for copy in started:
        copy.wait_send()


def per_device(nx, ny, positions, polarity, direct_field, atom_count, pair_list, pair_count):
    blocks, atoms = positions.shape[2], positions.shape[4]
    groups = atoms // ROWS
    comps = 6 * blocks
    vrows = -(-comps // 8) * 8
    links = 3 * blocks - 2
    names = -(-5 * blocks * blocks // 8) * 8
    f32 = jnp.float32
    vmem = pl.BlockSpec(memory_space=pltpu.VMEM)
    smem = pl.BlockSpec(memory_space=pltpu.SMEM)
    out = jax.ShapeDtypeStruct((blocks, 6, atoms), f32)
    sem = pltpu.SemaphoreType.DMA
    dipoles, residual = pl.pallas_call(
        functools.partial(kernel, nx, ny, blocks),
        out_shape=(out, out),
        in_specs=[smem, smem, vmem, vmem, vmem, vmem],
        out_specs=(vmem, vmem),
        scratch_shapes=[
            pltpu.VMEM((GEO_ROWS + vrows, atoms), f32),
            pltpu.VMEM((4, GEO_ROWS, atoms), f32),
            pltpu.VMEM((vrows, atoms), f32),
            pltpu.VMEM((4, vrows, atoms), f32),
            pltpu.VMEM((4, GEO_ROWS + vrows, atoms), f32),
            pltpu.VMEM((vrows, atoms), f32),
            pltpu.VMEM((vrows, atoms), f32),
            pltpu.VMEM((vrows, atoms), f32),
            pltpu.VMEM((vrows, atoms), f32),
            pltpu.VMEM((names, atoms), f32),
            pltpu.VMEM((4 * blocks, atoms, atoms), f32),
            pltpu.VMEM((comps, atoms, atoms), f32),
            pltpu.VMEM((comps, atoms, atoms), f32),
            pltpu.VMEM((4, comps, 8, atoms), f32),
            pltpu.VMEM((comps, 8, atoms), f32),
            pltpu.VMEM((links * groups, 4, 4, ROWS, atoms), f32),
            pltpu.VMEM((blocks * groups, 4, ROWS, atoms), f32),
            pltpu.VMEM(((blocks - 1) * groups, 4, ROWS, atoms), f32),
            pltpu.VMEM((2, 4, vrows, atoms), f32),
            pltpu.VMEM((2, 4, vrows, atoms), f32),
            pltpu.VMEM((3, 2, 8, atoms), f32),
            pltpu.VMEM((3, nx - 1, 8, atoms), f32),
            pltpu.VMEM((3, ny - 1, 8, atoms), f32),
            sem((2, 4)),
            sem((2, 4)),
            sem((2, 4)),
            sem((2, 4)),
            sem((3, nx - 1)),
            sem((3, nx - 1)),
            sem((3, ny - 1)),
            sem((3, ny - 1)),
        ],
        compiler_params=pltpu.CompilerParams(
            collective_id=0, has_side_effects=True, vmem_limit_bytes=40 * 1024 * 1024
        ),
    )(
        atom_count[0],
        pair_count,
        positions[0, 0],
        polarity[0, 0],
        direct_field[0, 0],
        pair_list[0, 0],
    )
    return (dipoles[None, None], residual[None, None])


def solution(mesh):
    in_specs = (
        P("gx", "gy", None, None, None),
        P("gx", "gy", None, None),
        P("gx", "gy", None, None, None),
        P("gx", "gy", None),
        P("gx", "gy", None, None),
        P("gx", "gy"),
    )
    out_specs = (P("gx", "gy", None, None, None), P("gx", "gy", None, None, None))
    body = functools.partial(per_device, mesh.shape["gx"], mesh.shape["gy"])
    return jax.shard_map(
        body, mesh=mesh, in_specs=in_specs, out_specs=out_specs, check_vma=False
    )
```
